32 devices in a mesh: group: 4 (over y, core), fsdp: 8 (over z, x).
Axes of the slice: x: 2, y: 2, z: 4, core: 2. Of those that a mesh axis runs over, the one named last changes fastest.
Arguments:
- anchor: bfloat16 [8192, 1024], P('fsdp'), may hold values from -6 to 6
- pseudo_grads: bfloat16 [4, 8192, 1024], P('group', 'fsdp'), may hold values from -1.5 to 1.5
- outer_moment: float32 [8192, 1024], P('fsdp'), may hold values from -1.2 to 1.2
- adam_first: float32 [4, 8192, 1024], P('group', 'fsdp'), may hold values from -1.8 to 1.8
- adam_second: float32 [4, 8192, 1024], P('group', 'fsdp'), may hold values from 0.25 to 4
- inputs: bfloat16 [8192, 8192], P(('group', 'fsdp')), may hold values from -6 to 6
- key_cotangent: bfloat16 [8192, 1024], P(('group', 'fsdp')), may hold values from -6 to 6
Outputs:
- new_anchor: bfloat16 [8192, 1024], P('fsdp')
- new_moment: float32 [8192, 1024], P('fsdp')
- inner_weights: bfloat16 [4, 8192, 1024], P('group', 'fsdp')
- first_moment: float32 [4, 8192, 1024], P('group', 'fsdp')
- second_moment: float32 [4, 8192, 1024], P('group', 'fsdp')
- input_grad: bfloat16 [8192, 8192], P(('group', 'fsdp'))
The draws below stay inside these ranges and needn't reach their ends.
All inputs are finite; a program needn't handle non-finite values.
Results may differ from the reference program's by a relative error of at most 0.012.
Values may be sent and summed in bfloat16 or wider, within the bound.
A program may use at most 128 MiB of HBM per device.

```python
import math
import jax
import jax.numpy as jnp
from jax import lax

D = 8192
KV = 1024
TOK_DEV = 256
GROUPS = 4
TOKENS = 8192
N_GROUP = 4
N_FSDP = 8


def spiked(entries, key, source, target, parts, factor):
    def block_of(position):
        return (jnp.arange(entries.shape[position]) // (entries.shape[position] // parts)).reshape((-1,) + (1,) * (entries.ndim - 1 - position))

    one_side = jax.random.permutation(key, parts)[block_of(target)]
    other_side = (block_of(target) + parts // 2) % parts
    return jnp.where((block_of(source) == one_side) | (block_of(source) == other_side), factor * entries, entries)


def shard_levels(key, shape, shards, low, top_value):
    loudness = 1.0
    for axis_at, parts in shards:
        steps = jax.random.uniform(jax.random.fold_in(jax.random.fold_in(key, 6), axis_at), (parts,), jnp.float32, low / len(shards), top_value / len(shards))
        loudness = loudness * jnp.repeat(jnp.exp(steps), shape[axis_at] // parts).reshape((-1,) + (1,) * (len(shape) - 1 - axis_at))
    return loudness


def scatter_about(own_key, extent, spread, reach, shards=(), dtype=jnp.bfloat16):
    gain = shard_levels(own_key, extent, shards, -0.22, 0.18) if shards else 1.0
    entries = jax.random.normal(own_key, extent, jnp.float32) * spread * gain
    return jnp.minimum(jnp.maximum(entries, -reach), reach).astype(dtype)


def noise_with(stream_key, extent, scale, limit, split, heavy, dtype=jnp.bfloat16):
    values = scale * jax.random.normal(stream_key, extent, jnp.float32)
    if split:
        values = values * shard_levels(stream_key, extent, split, -0.22, 0.18)
    return jnp.clip(spiked(values, jax.random.fold_in(stream_key, 3), *heavy), -limit, limit).astype(dtype)


def setup_inputs(seed: int = 0) -> dict:
    key_of = jax.random.split(jax.random.key(seed), 8)
    anchor = scatter_about(key_of[0], (D, KV), 1.0, 6.0, ((0, 8),))
    pseudo_grads = scatter_about(key_of[1], (GROUPS, D, KV), 0.25, 1.5, ((0, 4), (1, 8)))
    outer_moment = scatter_about(key_of[2], (D, KV), 0.2, 1.2, ((0, 8),), jnp.float32)
    adam_first = scatter_about(key_of[3], (GROUPS, D, KV), 0.3, 1.8, ((0, 4), (1, 8)), jnp.float32)
    adam_second = jnp.clip(jnp.exp(math.log(4.0) - 2.7725887 * jax.random.uniform(key_of[4], (GROUPS, D, KV), jnp.float32) ** shard_levels(key_of[4], (GROUPS, D, KV), ((0, 4), (1, 8)), -0.2, 0.2)), 0.25, 4.0)
    inputs = noise_with(key_of[5], (TOKENS, D), 1.0, 6.0, ((0, 32),), (0, 1, 32, 2.75))
    key_cotangent = scatter_about(key_of[6], (TOKENS, KV), 1.0, 6.0, ((0, 32),))
    return dict(anchor=anchor, pseudo_grads=pseudo_grads, outer_moment=outer_moment, adam_first=adam_first, adam_second=adam_second, inputs=inputs, key_cotangent=key_cotangent)


OUTER_RATE = 0.7
MOMENTUM = 0.9
INNER_RATE = 0.05
BETA_ONE = 0.9
BETA_TWO = 0.95
ADAM_EPS = 1e-08
DECAY = 0.1
ADAM_STEP = 100

def reference(anchor, pseudo_grads, outer_moment, adam_first, adam_second, inputs, key_cotangent):
    scale = D ** (-0.5)
    mean_delta = lax.optimization_barrier(jnp.sum(pseudo_grads.astype(jnp.float32), axis=0)) / N_GROUP
    new_moment = MOMENTUM * outer_moment + mean_delta
    new_anchor = (anchor.astype(jnp.float32) - OUTER_RATE * (mean_delta + MOMENTUM * new_moment)).astype(jnp.bfloat16)
    cot_blocks = key_cotangent.reshape(N_GROUP * N_FSDP, TOK_DEV, KV)

    def input_block(block):
        return (jnp.dot(block, new_anchor.T, preferred_element_type=jnp.float32) * scale).astype(jnp.bfloat16)
    input_grad = lax.map(input_block, cot_blocks).reshape(N_GROUP * N_FSDP * TOK_DEV, D)
    in_blocks = inputs.reshape(N_GROUP, N_FSDP, TOK_DEV, D)
    cot_groups = key_cotangent.reshape(N_GROUP, N_FSDP, TOK_DEV, KV)

    def worker(pair):
        x_worker, k_worker = pair

        def add_block(total, block):
            x_block, k_block = block
            part = (jnp.dot(x_block.T, k_block, preferred_element_type=jnp.float32) * scale).astype(jnp.bfloat16)
            part = lax.optimization_barrier(part)
            return (total + part.astype(jnp.float32), None)
        total, unused = lax.scan(add_block, jnp.zeros((D, KV), jnp.float32), (x_worker, k_worker))
        return total
    grads = lax.map(worker, (in_blocks, cot_groups))
    correct_one = 1.0 - BETA_ONE ** ADAM_STEP
    correct_two = 1.0 - BETA_TWO ** ADAM_STEP
    first_moment = BETA_ONE * adam_first + (1.0 - BETA_ONE) * grads
    second_moment = BETA_TWO * adam_second + (1.0 - BETA_TWO) * grads * grads
    base = new_anchor.astype(jnp.float32)[None]
    step_size = first_moment / correct_one / (jnp.sqrt(second_moment / correct_two) + ADAM_EPS)
    inner_weights = (base * (1.0 - INNER_RATE * DECAY) - INNER_RATE * step_size).astype(jnp.bfloat16)
    return (new_anchor, new_moment, inner_weights, first_moment, second_moment, input_grad)
```

```python
import functools

import jax
import jax.numpy as jnp
from jax import lax
from jax.experimental import pallas as pl
from jax.experimental.pallas import tpu as pltpu
from jax.sharding import PartitionSpec as P

OUTER_RATE = 0.7
MOMENTUM = 0.9
INNER_RATE = 0.05
BETA_ONE = 0.9
BETA_TWO = 0.95
ADAM_EPS = 1e-08
DECAY = 0.1
ADAM_STEP = 100

TILE = 256
MESH = pl.DeviceIdType.MESH


def ring_to_index(place, n):
    back = lax.div(place, n // 2)
    return (1 - back) * 2 * place + back * (2 * n - 1 - 2 * place)


def index_to_ring(index, n):
    column = lax.rem(index, 2)
    row = lax.div(index, 2)
    return (1 - column) * row + column * (n - 1 - row)


def exchange_kernel(
    n, scale,
    pg, anchor, moment, inputs, cot,
    grads, mean_out, input_grad,
    rows_in, cots, anchors, pg_in, pg_own, anchor_own, moment_own, means,
    local_sem,
    pg_send, pg_recv, x_send, x_recv, cot_send, cot_recv, ring_send, ring_recv,
    y_send, y_recv, core_send, core_recv, pass_send, pass_recv, mean_send, mean_recv,
):
    half = n // 2
    tokens = inputs.shape[0]
    shard = anchor.shape[0]
    part = shard // 4
    me = lax.axis_index("fsdp")
    mine = lax.axis_index("group")
    place = index_to_ring(me, n)
    right = ring_to_index(lax.rem(place + 1, n), n)
    left = ring_to_index(lax.rem(place + n - 1, n), n)
    y, core = lax.div(mine, 2), lax.rem(mine, 2)
    core_peer = 2 * y + 1 - core
    y_peer = 2 * (1 - y) + core
    far_peer = 2 * (1 - y) + 1 - core
    peers = (core_peer, y_peer, far_peer)

    def owner(slot):
        return ring_to_index(lax.rem(place + n - slot, n), n)

    def quarter(which):
        return pl.ds(pl.multiple_of(which * part, part), part)

    def local(src, dst, sem):
        return pltpu.make_async_copy(src, dst, local_sem.at[sem])

    def remote(src, dst, send, recv, fsdp, group):
        return pltpu.make_async_remote_copy(
            src_ref=src, dst_ref=dst, send_sem=send, recv_sem=recv,
            device_id={"group": group, "fsdp": fsdp}, device_id_type=MESH,
        )

    def shard_columns(index):
        return pl.ds(pl.multiple_of(index * shard, shard), shard)

    own_copies = [
        local(cot, cots.at[0], 0),
        local(pg.at[0, quarter(mine), :], pg_own, 1),
        local(anchor.at[quarter(mine), :], anchor_own, 2),
        local(moment.at[quarter(mine), :], moment_own, 3),
        local(inputs.at[:, shard_columns(me)], rows_in.at[0], 4),
    ]
    for copy in own_copies:
        copy.start()

    barrier = pltpu.get_barrier_semaphore()
    for step in range(1, n):
        pl.semaphore_signal(
            barrier, inc=1, device_id={"group": mine, "fsdp": owner(step)}, device_id_type=MESH
        )
    for peer in peers:
        pl.semaphore_signal(
            barrier, inc=1, device_id={"group": peer, "fsdp": me}, device_id_type=MESH
        )
    pl.semaphore_wait(barrier, n + 2)

    sent = []

    def send(copy):
        copy.start()
        sent.append(copy)

    pg_copies = [
        remote(pg.at[0, quarter(peer), :], pg_in.at[i], pg_send.at[i], pg_recv.at[i], me, peer)
        for i, peer in enumerate(peers)
    ]
    for i in (1, 2, 0):
        send(pg_copies[i])

    def ring_step(buffer, rows, first, step, send_sem, recv_sem):
        if step < half:
            spans = ((first, rows, step), (first, rows, n - step))
        else:
            spans = ((first, rows // 2, half), (first + rows // 2, rows // 2, n))
        (up, up_rows, up_sem), (down, down_rows, down_sem) = spans
        up_at = pl.ds(pl.multiple_of(up, rows // 2), up_rows)
        down_at = pl.ds(pl.multiple_of(down, rows // 2), down_rows)
        return (
            remote(
                buffer.at[step - 1, up_at, :], buffer.at[step, up_at, :],
                send_sem.at[up_sem], recv_sem.at[up_sem], right, mine,
            ),
            remote(
                buffer.at[(n - step + 1) % n, down_at, :], buffer.at[n - step, down_at, :],
                send_sem.at[down_sem], recv_sem.at[down_sem], left, mine,
            ),
        )

    cot_steps = [None] + [
        ring_step(cots, tokens, 0, step, cot_send, cot_recv) for step in range(1, half + 1)
    ]
    ring_steps = [None] + [
        ring_step(anchors, part, mine * part, step, ring_send, ring_recv)
        for step in range(1, half + 1)
    ]

    own_copies[0].wait()
    for copy in cot_steps[1]:
        send(copy)

    x_copies = [None] * n
    for step in range(1, half + 1):
        for slot in (step, n - step) if step < half else (half,):
            target = ring_to_index(lax.rem(place + slot, n), n)
            x_copies[slot] = remote(
                inputs.at[:, shard_columns(target)], rows_in.at[slot],
                x_send.at[slot], x_recv.at[slot], target, mine,
            )
            send(x_copies[slot])

    def cot_turn(step):
        for copy in cot_steps[step]:
            copy.wait_recv()
        if step < half:
            for copy in cot_steps[step + 1]:
                send(copy)

    def slots_of(step):
        if step == 0:
            return (0,)
        return (step, n - step) if step < half else (half,)

    def over(slot, which, send_sem, recv_sem, peer):
        view = anchors.at[slot, quarter(which), :]
        return remote(view, view, send_sem.at[slot], recv_sem.at[slot], me, peer)

    def spread(step):
        for slot in slots_of(step):
            send(over(slot, mine, y_send, y_recv, y_peer))
            send(over(slot, mine, core_send, core_recv, core_peer))

    def hand_on(step):
        for slot in slots_of(step):
            over(slot, mine, y_send, y_recv, y_peer).wait_recv()
            send(over(slot, y_peer, pass_send, pass_recv, core_peer))

    def mean_copy(which, i, peer):
        view = means.at[quarter(which), :]
        return remote(view, view, mean_send.at[i], mean_recv.at[i], me, peer)

    def add_grads(slot):
        if slot == 0:
            own_copies[4].wait()
        else:
            x_copies[slot].wait_recv()

        @pl.loop(0, shard // TILE)
        def _(tile):
            at = pl.ds(pl.multiple_of(tile * TILE, TILE), TILE)
            term = lax.dot_general(
                rows_in[slot, :, at], cots[slot], (((0,), (0,)), ((), ())),
                preferred_element_type=jnp.float32,
            )
            if slot == 0:
                grads[at, :] = term
            else:
                grads[at, :] += term

    def put_input_grad(slot):
        over(slot, mine, core_send, core_recv, core_peer).wait_recv()
        over(slot, y_peer, pass_send, pass_recv, core_peer).wait_recv()
        base = owner(slot) * shard

        @pl.loop(0, shard // TILE)
        def _(tile):
            at = pl.ds(pl.multiple_of(tile * TILE, TILE), TILE)
            term = lax.dot_general(
                cots[0], anchors[slot, at, :], (((1,), (1,)), ((), ())),
                preferred_element_type=jnp.float32,
            )
            columns = pl.ds(pl.multiple_of(base + tile * TILE, TILE), TILE)
            input_grad[:, columns] = (term * scale).astype(input_grad.dtype)

    cot_turn(1)

    for copy in own_copies[1:4]:
        copy.wait()
    for copy in pg_copies:
        copy.wait_recv()

    chunk = 32

    @pl.loop(0, part // chunk)
    def _(i):
        at = pl.ds(pl.multiple_of(i * chunk, chunk), chunk)
        to = pl.ds(pl.multiple_of(mine * part + i * chunk, chunk), chunk)
        total = pg_own[at, :].astype(jnp.float32)
        for peer in range(3):
            total += pg_in[peer, at, :].astype(jnp.float32)
        mean = total / 4
        moved = MOMENTUM * moment_own[at, :] + mean
        updated = anchor_own[at, :].astype(jnp.float32) - OUTER_RATE * (mean + MOMENTUM * moved)
        anchors[0, to, :] = updated.astype(anchors.dtype)
        means[to, :] = mean.astype(means.dtype)

    for copy in ring_steps[1]:
        send(copy)
    spread(0)
    send(mean_copy(mine, 0, core_peer))
    send(mean_copy(mine, 1, y_peer))
    add_grads(0)

    for step in range(1, half + 1):
        for copy in ring_steps[step]:
            copy.wait_recv()
        if step < half:
            for copy in ring_steps[step + 1]:
                send(copy)
        spread(step)
        if step < half:
            cot_turn(step + 1)
        hand_on(step - 1)
        if step == 1:
            mean_copy(mine, 1, y_peer).wait_recv()
            send(mean_copy(y_peer, 2, core_peer))
        if step >= 2:
            for slot in slots_of(step - 2):
                put_input_grad(slot)
            for slot in slots_of(step - 1):
                add_grads(slot)

    for slot in slots_of(half - 1):
        put_input_grad(slot)
    mean_copy(mine, 0, core_peer).wait_recv()
    mean_copy(y_peer, 2, core_peer).wait_recv()

    @pl.loop(0, shard // chunk)
    def _(i):
        at = pl.ds(pl.multiple_of(i * chunk, chunk), chunk)
        mean_out[at, :] = means[at, :]

    for slot in slots_of(half):
        add_grads(slot)
    hand_on(half)
    for slot in slots_of(half):
        put_input_grad(slot)
    for copy in sent:
        copy.wait_send()


def exchange(n, scale, pg, anchor, moment, inputs, cot):
    tokens, width = inputs.shape
    shard, keys = anchor.shape
    part = shard // 4
    bf16, f32 = jnp.bfloat16, jnp.float32
    sem = pltpu.SemaphoreType.DMA
    return pl.pallas_call(
        functools.partial(exchange_kernel, n, scale),
        out_shape=(
            jax.ShapeDtypeStruct((shard, keys), f32),
            jax.ShapeDtypeStruct((shard, keys), bf16),
            jax.ShapeDtypeStruct((tokens, width), bf16),
        ),
        in_specs=[pl.BlockSpec(memory_space=pl.ANY)] * 5,
        out_specs=(pl.BlockSpec(memory_space=pltpu.VMEM),) * 3,
        scratch_shapes=[
            pltpu.VMEM((n, tokens, shard), bf16),
            pltpu.VMEM((n, tokens, keys), bf16),
            pltpu.VMEM((n, shard, keys), bf16),
            pltpu.VMEM((3, part, keys), bf16),
            pltpu.VMEM((part, keys), bf16),
            pltpu.VMEM((part, keys), bf16),
            pltpu.VMEM((part, keys), f32),
            pltpu.VMEM((shard, keys), bf16),
            sem((5,)),
            sem((3,)), sem((3,)),
            sem((n,)), sem((n,)),
            sem((n + 1,)), sem((n + 1,)),
            sem((n + 1,)), sem((n + 1,)),
            sem((n,)), sem((n,)),
            sem((n,)), sem((n,)),
            sem((n,)), sem((n,)),
            sem((3,)), sem((3,)),
        ],
        compiler_params=pltpu.CompilerParams(
            collective_id=0, has_side_effects=True, vmem_limit_bytes=58 * 2**20
        ),
        cost_estimate=pl.CostEstimate(
            flops=4 * tokens * width * keys,
            bytes_accessed=2 * (2 * tokens * width + 4 * shard * keys),
            transcendentals=0,
        ),
    )(pg, anchor, moment, inputs, cot)


def per_device(anchor, pseudo_grads, outer_moment, adam_first, adam_second, inputs, key_cotangent):
    scale = inputs.shape[1] ** (-0.5)
    raw, mean, input_grad = exchange(
        lax.axis_size("fsdp"), scale, pseudo_grads, anchor, outer_moment, inputs, key_cotangent
    )
    mean_delta = mean.astype(jnp.float32)
    grads = raw * scale
    new_moment = MOMENTUM * outer_moment + mean_delta
    new_anchor = (
        anchor.astype(jnp.float32) - OUTER_RATE * (mean_delta + MOMENTUM * new_moment)
    ).astype(jnp.bfloat16)
    correct_one = 1.0 - BETA_ONE**ADAM_STEP
    correct_two = 1.0 - BETA_TWO**ADAM_STEP
    first_moment = BETA_ONE * adam_first[0] + (1.0 - BETA_ONE) * grads
    second_moment = BETA_TWO * adam_second[0] + (1.0 - BETA_TWO) * grads * grads
    step_size = first_moment / correct_one / (jnp.sqrt(second_moment / correct_two) + ADAM_EPS)
    inner_weights = (
        new_anchor.astype(jnp.float32) * (1.0 - INNER_RATE * DECAY) - INNER_RATE * step_size
    ).astype(jnp.bfloat16)
    return (
        new_anchor,
        new_moment,
        inner_weights[None],
        first_moment[None],
        second_moment[None],
        input_grad,
    )


def solution(mesh):
    return jax.shard_map(
        per_device,
        mesh=mesh,
        in_specs=(
            P("fsdp", None),
            P("group", "fsdp", None),
            P("fsdp", None),
            P("group", "fsdp", None),
            P("group", "fsdp", None),
            P(("group", "fsdp"), None),
            P(("group", "fsdp"), None),
        ),
        out_specs=(
            P("fsdp", None),
            P("fsdp", None),
            P("group", "fsdp", None),
            P("group", "fsdp", None),
            P("group", "fsdp", None),
            P(("group", "fsdp"), None),
        ),
        check_vma=False,
    )
```

```python
import functools

import jax
import jax.numpy as jnp
from jax import lax
from jax.experimental import pallas as pl
from jax.experimental.pallas import tpu as pltpu
from jax.sharding import PartitionSpec as P

OUTER_RATE = 0.7
MOMENTUM = 0.9
INNER_RATE = 0.05
BETA_ONE = 0.9
BETA_TWO = 0.95
ADAM_EPS = 1e-08
DECAY = 0.1
ADAM_STEP = 100

TILE = 256
MESH = pl.DeviceIdType.MESH


def flip(index, slot):
    bit = 1
    while bit <= slot:
        if slot & bit:
            index = index + bit * (1 - 2 * lax.rem(lax.div(index, bit), 2))
        bit *= 2
    return index


def children(slot, n):
    top = slot & -slot if slot else n
    return [slot | 1 << at for at in reversed(range(n.bit_length() - 1)) if 1 << at < top]


def level_slots(level, n):
    return [slot for slot in range(n) if bin(slot).count("1") == level]


def exchange_kernel(
    n, scale,
    pg, anchor, moment, inputs, cot,
    grads, mean_out, input_grad,
    rows_in, cots, anchors, pg_in, pg_own, anchor_own, moment_own, means,
    local_sem,
    pg_send, pg_recv, x_send, x_recv, cot_send, cot_recv, tree_send, tree_recv,
    y_send, y_recv, core_send, core_recv, pass_send, pass_recv, mean_send, mean_recv,
):
    levels = n.bit_length() - 1
    tokens = inputs.shape[0]
    shard = anchor.shape[0]
    part = shard // 4
    me = lax.axis_index("fsdp")
    mine = lax.axis_index("group")
    y, core = lax.div(mine, 2), lax.rem(mine, 2)
    core_peer = 2 * y + 1 - core
    y_peer = 2 * (1 - y) + core
    far_peer = 2 * (1 - y) + 1 - core
    peers = (core_peer, y_peer, far_peer)

    def owner(slot):
        return flip(me, slot)

    def quarter(which):
        return pl.ds(pl.multiple_of(which * part, part), part)

    def local(src, dst, sem):
        return pltpu.make_async_copy(src, dst, local_sem.at[sem])

    def remote(src, dst, send, recv, fsdp, group):
        return pltpu.make_async_remote_copy(
            src_ref=src, dst_ref=dst, send_sem=send, recv_sem=recv,
            device_id={"group": group, "fsdp": fsdp}, device_id_type=MESH,
        )

    def shard_columns(index):
        return pl.ds(pl.multiple_of(index * shard, shard), shard)

    own_copies = [
        local(cot, cots.at[0], 0),
        local(pg.at[0, quarter(mine), :], pg_own, 1),
        local(anchor.at[quarter(mine), :], anchor_own, 2),
        local(moment.at[quarter(mine), :], moment_own, 3),
        local(inputs.at[:, shard_columns(me)], rows_in.at[0], 4),
    ]
    for copy in own_copies:
        copy.start()

    barrier = pltpu.get_barrier_semaphore()
    for step in range(1, n):
        pl.semaphore_signal(
            barrier, inc=1, device_id={"group": mine, "fsdp": owner(step)}, device_id_type=MESH
        )
    for peer in peers:
        pl.semaphore_signal(
            barrier, inc=1, device_id={"group": peer, "fsdp": me}, device_id_type=MESH
        )
    pl.semaphore_wait(barrier, n + 2)

    sent = []

    def send(copy):
        copy.start()
        sent.append(copy)

    pg_copies = [
        remote(pg.at[0, quarter(peer), :], pg_in.at[i], pg_send.at[i], pg_recv.at[i], me, peer)
        for i, peer in enumerate(peers)
    ]
    for i in (1, 2, 0):
        send(pg_copies[i])

    def tree_copy(buffer, rows, slot, child, send_sem, recv_sem):
        return remote(
            buffer.at[slot, rows, :], buffer.at[child, rows, :],
            send_sem.at[child], recv_sem.at[child], flip(me, child - slot), mine,
        )

    def parent(slot):
        return slot & (slot - 1)

    def cot_copy(child):
        return tree_copy(cots, pl.ds(0, tokens), parent(child), child, cot_send, cot_recv)

    def anchor_copy(child):
        return tree_copy(anchors, quarter(mine), parent(child), child, tree_send, tree_recv)

    own_copies[0].wait()
    for child in children(0, n):
        send(cot_copy(child))

    def x_copy(slot):
        target = owner(slot)
        return remote(
            inputs.at[:, shard_columns(target)], rows_in.at[slot],
            x_send.at[slot], x_recv.at[slot], target, mine,
        )

    order = sorted(range(1, n), reverse=True)
    early = [slot for slot in order if bin(slot).count("1") < 2 or slot == n // 2 + 1]
    for slot in early:
        send(x_copy(slot))

    def cot_turn(level):
        for slot in level_slots(level, n):
            cot_copy(slot).wait_recv()
            for child in children(slot, n):
                send(cot_copy(child))

    def over(slot, which, send_sem, recv_sem, peer):
        view = anchors.at[slot, quarter(which), :]
        return remote(view, view, send_sem.at[slot], recv_sem.at[slot], me, peer)

    def spread(slot):
        send(over(slot, mine, y_send, y_recv, y_peer))
        send(over(slot, mine, core_send, core_recv, core_peer))

    def hand_on(level):
        for slot in level_slots(level, n):
            over(slot, mine, y_send, y_recv, y_peer).wait_recv()
            send(over(slot, y_peer, pass_send, pass_recv, core_peer))

    def mean_copy(which, i, peer):
        view = means.at[quarter(which), :]
        return remote(view, view, mean_send.at[i], mean_recv.at[i], me, peer)

    def add_grads(slot):
        if slot == 0:
            own_copies[4].wait()
        else:
            x_copy(slot).wait_recv()

        @pl.loop(0, shard // TILE)
        def _(tile):
            at = pl.ds(pl.multiple_of(tile * TILE, TILE), TILE)
            term = lax.dot_general(
                rows_in[slot, :, at], cots[slot], (((0,), (0,)), ((), ())),
                preferred_element_type=jnp.float32,
            )
            if slot == 0:
                grads[at, :] = term
            else:
                grads[at, :] += term

    def put_input_grad(slot):
        over(slot, mine, core_send, core_recv, core_peer).wait_recv()
        over(slot, y_peer, pass_send, pass_recv, core_peer).wait_recv()
        base = owner(slot) * shard

        @pl.loop(0, shard // TILE)
        def _(tile):
            at = pl.ds(pl.multiple_of(tile * TILE, TILE), TILE)
            term = lax.dot_general(
                cots[0], anchors[slot, at, :], (((1,), (1,)), ((), ())),
                preferred_element_type=jnp.float32,
            )
            columns = pl.ds(pl.multiple_of(base + tile * TILE, TILE), TILE)
            input_grad[:, columns] = (term * scale).astype(input_grad.dtype)

    for copy in own_copies[1:4]:
        copy.wait()
    for copy in pg_copies:
        copy.wait_recv()

    chunk = 32

    @pl.loop(0, part // chunk)
    def _(i):
        at = pl.ds(pl.multiple_of(i * chunk, chunk), chunk)
        to = pl.ds(pl.multiple_of(mine * part + i * chunk, chunk), chunk)
        total = pg_own[at, :].astype(jnp.float32)
        for peer in range(3):
            total += pg_in[peer, at, :].astype(jnp.float32)
        mean = total / 4
        moved = MOMENTUM * moment_own[at, :] + mean
        updated = anchor_own[at, :].astype(jnp.float32) - OUTER_RATE * (mean + MOMENTUM * moved)
        anchors[0, to, :] = updated.astype(anchors.dtype)
        means[to, :] = mean.astype(means.dtype)

    for child in children(0, n):
        send(anchor_copy(child))
    spread(0)
    cot_turn(1)

    for level in range(1, levels + 1):
        for slot in level_slots(level, n):
            anchor_copy(slot).wait_recv()
            for child in children(slot, n):
                send(anchor_copy(child))
            spread(slot)
        if level == 1:
            for slot in order:
                if slot not in early:
                    send(x_copy(slot))
            send(mean_copy(mine, 0, core_peer))
            send(mean_copy(mine, 1, y_peer))
        if level < levels:
            cot_turn(level + 1)
        hand_on(level - 1)
        if level == 1:
            add_grads(0)
        if level == 2:
            mean_copy(mine, 1, y_peer).wait_recv()
            send(mean_copy(y_peer, 2, core_peer))
        if level >= 2:
            for slot in level_slots(level - 2, n):
                put_input_grad(slot)
        if level == 2:
            for slot in level_slots(1, n)[:2]:
                add_grads(slot)

    late = [slot for slot in range(1, n) if slot not in level_slots(1, n)[:2]]
    for slot in late[: len(late) // 2]:
        add_grads(slot)
    for slot in level_slots(levels - 1, n):
        put_input_grad(slot)
    mean_copy(mine, 0, core_peer).wait_recv()
    mean_copy(y_peer, 2, core_peer).wait_recv()

    @pl.loop(0, shard // chunk)
    def _(i):
        at = pl.ds(pl.multiple_of(i * chunk, chunk), chunk)
        mean_out[at, :] = means[at, :]

    hand_on(levels)
    for slot in late[len(late) // 2 :]:
        add_grads(slot)
    put_input_grad(n - 1)
    for copy in sent:
        copy.wait_send()


def exchange(n, scale, pg, anchor, moment, inputs, cot):
    tokens, width = inputs.shape
    shard, keys = anchor.shape
    part = shard // 4
    bf16, f32 = jnp.bfloat16, jnp.float32
    sem = pltpu.SemaphoreType.DMA
    return pl.pallas_call(
        functools.partial(exchange_kernel, n, scale),
        out_shape=(
            jax.ShapeDtypeStruct((shard, keys), f32),
            jax.ShapeDtypeStruct((shard, keys), bf16),
            jax.ShapeDtypeStruct((tokens, width), bf16),
        ),
        in_specs=[pl.BlockSpec(memory_space=pl.ANY)] * 5,
        out_specs=(pl.BlockSpec(memory_space=pltpu.VMEM),) * 3,
        scratch_shapes=[
            pltpu.VMEM((n, tokens, shard), bf16),
            pltpu.VMEM((n, tokens, keys), bf16),
            pltpu.VMEM((n, shard, keys), bf16),
            pltpu.VMEM((3, part, keys), bf16),
            pltpu.VMEM((part, keys), bf16),
            pltpu.VMEM((part, keys), bf16),
            pltpu.VMEM((part, keys), f32),
            pltpu.VMEM((shard, keys), bf16),
            sem((5,)),
            sem((3,)), sem((3,)),
            sem((n,)), sem((n,)),
            sem((n,)), sem((n,)),
            sem((n,)), sem((n,)),
            sem((n,)), sem((n,)),
            sem((n,)), sem((n,)),
            sem((n,)), sem((n,)),
            sem((3,)), sem((3,)),
        ],
        compiler_params=pltpu.CompilerParams(
            collective_id=0, has_side_effects=True, vmem_limit_bytes=58 * 2**20
        ),
        cost_estimate=pl.CostEstimate(
            flops=4 * tokens * width * keys,
            bytes_accessed=2 * (2 * tokens * width + 4 * shard * keys),
            transcendentals=0,
        ),
    )(pg, anchor, moment, inputs, cot)


def per_device(anchor, pseudo_grads, outer_moment, adam_first, adam_second, inputs, key_cotangent):
    scale = inputs.shape[1] ** (-0.5)
    raw, mean, input_grad = exchange(
        lax.axis_size("fsdp"), scale, pseudo_grads, anchor, outer_moment, inputs, key_cotangent
    )
    mean_delta = mean.astype(jnp.float32)
    grads = raw * scale
    new_moment = MOMENTUM * outer_moment + mean_delta
    new_anchor = (
        anchor.astype(jnp.float32) - OUTER_RATE * (mean_delta + MOMENTUM * new_moment)
    ).astype(jnp.bfloat16)
    correct_one = 1.0 - BETA_ONE**ADAM_STEP
    correct_two = 1.0 - BETA_TWO**ADAM_STEP
    first_moment = BETA_ONE * adam_first[0] + (1.0 - BETA_ONE) * grads
    second_moment = BETA_TWO * adam_second[0] + (1.0 - BETA_TWO) * grads * grads
    step_size = first_moment / correct_one / (jnp.sqrt(second_moment / correct_two) + ADAM_EPS)
    inner_weights = (
        new_anchor.astype(jnp.float32) * (1.0 - INNER_RATE * DECAY) - INNER_RATE * step_size
    ).astype(jnp.bfloat16)
    return (
        new_anchor,
        new_moment,
        inner_weights[None],
        first_moment[None],
        second_moment[None],
        input_grad,
    )


def solution(mesh):
    return jax.shard_map(
        per_device,
        mesh=mesh,
        in_specs=(
            P("fsdp", None),
            P("group", "fsdp", None),
            P("fsdp", None),
            P("group", "fsdp", None),
            P("group", "fsdp", None),
            P(("group", "fsdp"), None),
            P(("group", "fsdp"), None),
        ),
        out_specs=(
            P("fsdp", None),
            P("fsdp", None),
            P("group", "fsdp", None),
            P("group", "fsdp", None),
            P("group", "fsdp", None),
            P(("group", "fsdp"), None),
        ),
        check_vma=False,
    )
```

```python
import functools

import jax
import jax.numpy as jnp
from jax import lax
from jax.experimental import pallas as pl
from jax.experimental.pallas import tpu as pltpu
from jax.sharding import PartitionSpec as P

OUTER_RATE = 0.7
MOMENTUM = 0.9
INNER_RATE = 0.05
BETA_ONE = 0.9
BETA_TWO = 0.95
ADAM_EPS = 1e-08
DECAY = 0.1
ADAM_STEP = 100

TILE = 256
PIECES = 2
MESH = pl.DeviceIdType.MESH


def flip(index, slot):
    bit = 1
    while bit <= slot:
        if slot & bit:
            index = index + bit * (1 - 2 * lax.rem(lax.div(index, bit), 2))
        bit *= 2
    return index


def children(slot, n):
    top = slot & -slot if slot else n
    return [slot | 1 << at for at in reversed(range(n.bit_length() - 1)) if 1 << at < top]


def level_slots(level, n):
    return [slot for slot in range(n) if bin(slot).count("1") == level]


def exchange_kernel(
    n, scale,
    pg, anchor, moment, inputs, cot,
    grads_out, mean_out, input_grad_out,
    grads, input_grad,
    rows_in, cots, anchors, pg_core, pg_y, pg_pair, pg_own, anchor_own, moment_own, means,
    local_sem, out_sem,
    pg_send, pg_recv, x_send, x_recv, cot_send, cot_recv, tree_send, tree_recv,
    y_send, y_recv, core_send, core_recv, pass_send, pass_recv, mean_send, mean_recv,
):
    levels = n.bit_length() - 1
    tokens = inputs.shape[0]
    shard = anchor.shape[0]
    part = shard // 4
    me = lax.axis_index("fsdp")
    mine = lax.axis_index("group")
    y, core = lax.div(mine, 2), lax.rem(mine, 2)
    core_peer = 2 * y + 1 - core
    y_peer = 2 * (1 - y) + core
    piece_rows = part // PIECES

    def owner(slot):
        return flip(me, slot)

    def quarter(which):
        return pl.ds(pl.multiple_of(which * part, part), part)

    def piece_of(which, piece):
        return pl.ds(
            pl.multiple_of(which * part + piece * piece_rows, piece_rows), piece_rows
        )

    def local(src, dst, sem):
        return pltpu.make_async_copy(src, dst, local_sem.at[sem])

    def remote(src, dst, send, recv, fsdp, group):
        return pltpu.make_async_remote_copy(
            src_ref=src, dst_ref=dst, send_sem=send, recv_sem=recv,
            device_id={"group": group, "fsdp": fsdp}, device_id_type=MESH,
        )

    def shard_columns(index):
        return pl.ds(pl.multiple_of(index * shard, shard), shard)

    own_copies = [
        local(cot, cots.at[0], 0),
        local(pg.at[0, quarter(mine), :], pg_own.at[0], 1),
        local(pg.at[0, quarter(y_peer), :], pg_own.at[1], 2),
        local(anchor.at[quarter(mine), :], anchor_own, 3),
        local(moment.at[quarter(mine), :], moment_own, 4),
        local(inputs.at[:, shard_columns(me)], rows_in.at[0], 5),
    ]
    for copy in own_copies:
        copy.start()

    barrier = pltpu.get_barrier_semaphore()
    for step in range(1, n):
        pl.semaphore_signal(
            barrier, inc=1, device_id={"group": mine, "fsdp": owner(step)}, device_id_type=MESH
        )
    for peer in (core_peer, y_peer):
        pl.semaphore_signal(
            barrier, inc=1, device_id={"group": peer, "fsdp": me}, device_id_type=MESH
        )
    pl.semaphore_wait(barrier, n + 1)

    sent = []

    def send(copy):
        copy.start()
        sent.append(copy)

    def pg_core_copy(i, theirs):
        return remote(
            pg.at[0, quarter(theirs), :], pg_core.at[i], pg_send.at[i], pg_recv.at[i],
            me, core_peer,
        )

    core_of_y = 2 * (1 - y) + 1 - core
    pg_copies = [pg_core_copy(0, core_peer), pg_core_copy(1, core_of_y)]
    for i in (1, 0):
        send(pg_copies[i])

    def tree_copy(buffer, rows, slot, child, send_sem, recv_sem):
        return remote(
            buffer.at[slot, rows, :], buffer.at[child, rows, :],
            send_sem.at[child], recv_sem.at[child], flip(me, child - slot), mine,
        )

    def parent(slot):
        return slot & (slot - 1)

    def cot_copy(child):
        return tree_copy(cots, pl.ds(0, tokens), parent(child), child, cot_send, cot_recv)

    def anchor_copy(child, piece):
        return tree_copy(
            anchors, piece_of(mine, piece), parent(child), child,
            tree_send.at[piece], tree_recv.at[piece],
        )

    own_copies[0].wait()
    for child in children(0, n):
        send(cot_copy(child))

    def x_copy(slot):
        target = owner(slot)
        return remote(
            inputs.at[:, shard_columns(target)], rows_in.at[slot],
            x_send.at[slot], x_recv.at[slot], target, mine,
        )

    bulk = {
        0: level_slots(1, n)[::-1],
        1: [slot for slot in level_slots(2, n)[::-1] if slot >= n // 2],
    }
    bulk[2] = [slot for slot in range(n - 1, 0, -1) if slot not in bulk[0] + bulk[1]]

    def send_bulk(turn):
        for slot in bulk[turn]:
            send(x_copy(slot))

    chunk = 32

    own_copies[2].wait()
    pg_copies[1].wait_recv()

    @pl.loop(0, part // chunk)
    def _(i):
        at = pl.ds(pl.multiple_of(i * chunk, chunk), chunk)
        pair = pg_own[1, at, :].astype(jnp.float32) + pg_core[1, at, :].astype(jnp.float32)
        pg_pair[at, :] = pair.astype(pg_pair.dtype)

    pg_y_copy = remote(pg_pair, pg_y, pg_send.at[2], pg_recv.at[2], me, y_peer)
    send(pg_y_copy)
    send_bulk(0)

    def cot_turn(level):
        for slot in level_slots(level, n):
            cot_copy(slot).wait_recv()
            for child in children(slot, n):
                send(cot_copy(child))

    def over(slot, piece, which, send_sem, recv_sem, peer):
        view = anchors.at[slot, piece_of(which, piece), :]
        return remote(view, view, send_sem.at[piece, slot], recv_sem.at[piece, slot], me, peer)

    def spread(slot, piece):
        send(over(slot, piece, mine, y_send, y_recv, y_peer))
        send(over(slot, piece, mine, core_send, core_recv, core_peer))

    def hand_on(level):
        for piece in range(PIECES):
            for slot in level_slots(level, n):
                over(slot, piece, mine, y_send, y_recv, y_peer).wait_recv()
                send(over(slot, piece, y_peer, pass_send, pass_recv, core_peer))

    def mean_copy(which, i, peer):
        view = means.at[quarter(which), :]
        return remote(view, view, mean_send.at[i], mean_recv.at[i], me, peer)

    out_copies = []

    def put_out(src, dst, at):
        copy = pltpu.make_async_copy(src, dst, out_sem.at[at])
        copy.start()
        out_copies.append(copy)

    def add_grads(slot):
        if slot == 0:
            own_copies[5].wait()
        else:
            x_copy(slot).wait_recv()

        @pl.loop(0, shard // TILE)
        def _(tile):
            at = pl.ds(pl.multiple_of(tile * TILE, TILE), TILE)
            term = lax.dot_general(
                rows_in[slot, :, at], cots[slot], (((0,), (0,)), ((), ())),
                preferred_element_type=jnp.float32,
            )
            if slot == 0:
                grads[at, :] = term
            else:
                grads[at, :] += term

    def put_input_grad(slot):
        for piece in range(PIECES):
            over(slot, piece, mine, core_send, core_recv, core_peer).wait_recv()
            over(slot, piece, y_peer, pass_send, pass_recv, core_peer).wait_recv()
        base = owner(slot) * shard

        @pl.loop(0, shard // TILE)
        def _(tile):
            at = pl.ds(pl.multiple_of(tile * TILE, TILE), TILE)
            term = lax.dot_general(
                cots[0], anchors[slot, at, :], (((1,), (1,)), ((), ())),
                preferred_element_type=jnp.float32,
            )
            columns = pl.ds(pl.multiple_of(base + tile * TILE, TILE), TILE)
            input_grad[:, columns] = (term * scale).astype(input_grad.dtype)

        put_out(
            input_grad.at[:, shard_columns(owner(slot))],
            input_grad_out.at[:, shard_columns(owner(slot))], slot,
        )

    for at in (1, 3, 4):
        own_copies[at].wait()
    pg_copies[0].wait_recv()
    pg_y_copy.wait_recv()

    @pl.loop(0, part // chunk)
    def _(i):
        at = pl.ds(pl.multiple_of(i * chunk, chunk), chunk)
        to = pl.ds(pl.multiple_of(mine * part + i * chunk, chunk), chunk)
        total = pg_own[0, at, :].astype(jnp.float32) + pg_core[0, at, :].astype(jnp.float32)
        mean = (total + pg_y[at, :].astype(jnp.float32)) / 4
        moved = MOMENTUM * moment_own[at, :] + mean
        updated = anchor_own[at, :].astype(jnp.float32) - OUTER_RATE * (mean + MOMENTUM * moved)
        anchors[0, to, :] = updated.astype(anchors.dtype)
        means[to, :] = mean.astype(means.dtype)

    for piece in range(PIECES):
        for child in children(0, n):
            send(anchor_copy(child, piece))
        spread(0, piece)
    send(mean_copy(mine, 0, core_peer))
    send(mean_copy(mine, 1, y_peer))
    cot_turn(1)

    late = level_slots(1, n)
    for level in range(1, levels + 1):
        for piece in range(PIECES):
            for slot in level_slots(level, n):
                anchor_copy(slot, piece).wait_recv()
                for child in children(slot, n):
                    send(anchor_copy(child, piece))
                spread(slot, piece)
        if level < 3:
            send_bulk(level)
        if level < levels:
            cot_turn(level + 1)
        hand_on(level - 1)
        if level == 1:
            add_grads(0)
            mean_copy(mine, 1, y_peer).wait_recv()
            send(mean_copy(y_peer, 2, core_peer))
        if level >= 2:
            for slot in level_slots(level - 2, n):
                put_input_grad(slot)
        if level == 2:
            for slot in late[:-1]:
                add_grads(slot)
        if level == 3:
            add_grads(late[-1])

    mean_copy(mine, 0, core_peer).wait_recv()
    mean_copy(y_peer, 2, core_peer).wait_recv()
    put_out(means, mean_out, n)
    for slot in bulk[1]:
        add_grads(slot)
    for slot in level_slots(levels - 1, n):
        put_input_grad(slot)
    hand_on(levels)
    for slot in bulk[2][::-1]:
        add_grads(slot)
    put_out(grads, grads_out, n + 1)
    put_input_grad(n - 1)
    for copy in sent:
        copy.wait_send()
    for copy in out_copies:
        copy.wait()


def exchange(n, scale, pg, anchor, moment, inputs, cot):
    tokens, width = inputs.shape
    shard, keys = anchor.shape
    part = shard // 4
    bf16, f32 = jnp.bfloat16, jnp.float32
    sem = pltpu.SemaphoreType.DMA
    return pl.pallas_call(
        functools.partial(exchange_kernel, n, scale),
        out_shape=(
            jax.ShapeDtypeStruct((shard, keys), f32),
            jax.ShapeDtypeStruct((shard, keys), bf16),
            jax.ShapeDtypeStruct((tokens, width), bf16),
        ),
        in_specs=[pl.BlockSpec(memory_space=pl.ANY)] * 5,
        out_specs=(pl.BlockSpec(memory_space=pl.ANY),) * 3,
        scratch_shapes=[
            pltpu.VMEM((shard, keys), f32),
            pltpu.VMEM((tokens, width), bf16),
            pltpu.VMEM((n, tokens, shard), bf16),
            pltpu.VMEM((n, tokens, keys), bf16),
            pltpu.VMEM((n, shard, keys), bf16),
            pltpu.VMEM((2, part, keys), bf16),
            pltpu.VMEM((part, keys), bf16),
            pltpu.VMEM((part, keys), bf16),
            pltpu.VMEM((2, part, keys), bf16),
            pltpu.VMEM((part, keys), bf16),
            pltpu.VMEM((part, keys), f32),
            pltpu.VMEM((shard, keys), bf16),
            sem((6,)), sem((n + 2,)),
            sem((3,)), sem((3,)),
            sem((n,)), sem((n,)),
            sem((n,)), sem((n,)),
            sem((PIECES, n)), sem((PIECES, n)),
            sem((PIECES, n)), sem((PIECES, n)),
            sem((PIECES, n)), sem((PIECES, n)),
            sem((PIECES, n)), sem((PIECES, n)),
            sem((3,)), sem((3,)),
        ],
        compiler_params=pltpu.CompilerParams(
            collective_id=0, has_side_effects=True, vmem_limit_bytes=58 * 2**20
        ),
        cost_estimate=pl.CostEstimate(
            flops=4 * tokens * width * keys,
            bytes_accessed=2 * (2 * tokens * width + 4 * shard * keys),
            transcendentals=0,
        ),
    )(pg, anchor, moment, inputs, cot)


def per_device(anchor, pseudo_grads, outer_moment, adam_first, adam_second, inputs, key_cotangent):
    scale = inputs.shape[1] ** (-0.5)
    raw, mean, input_grad = exchange(
        lax.axis_size("fsdp"), scale, pseudo_grads, anchor, outer_moment, inputs, key_cotangent
    )
    mean_delta = mean.astype(jnp.float32)
    grads = raw * scale
    new_moment = MOMENTUM * outer_moment + mean_delta
    new_anchor = (
        anchor.astype(jnp.float32) - OUTER_RATE * (mean_delta + MOMENTUM * new_moment)
    ).astype(jnp.bfloat16)
    correct_one = 1.0 - BETA_ONE**ADAM_STEP
    correct_two = 1.0 - BETA_TWO**ADAM_STEP
    first_moment = BETA_ONE * adam_first[0] + (1.0 - BETA_ONE) * grads
    second_moment = BETA_TWO * adam_second[0] + (1.0 - BETA_TWO) * grads * grads
    step_size = first_moment / correct_one / (jnp.sqrt(second_moment / correct_two) + ADAM_EPS)
    inner_weights = (
        new_anchor.astype(jnp.float32) * (1.0 - INNER_RATE * DECAY) - INNER_RATE * step_size
    ).astype(jnp.bfloat16)
    return (
        new_anchor,
        new_moment,
        inner_weights[None],
        first_moment[None],
        second_moment[None],
        input_grad,
    )


def solution(mesh):
    return jax.shard_map(
        per_device,
        mesh=mesh,
        in_specs=(
            P("fsdp", None),
            P("group", "fsdp", None),
            P("fsdp", None),
            P("group", "fsdp", None),
            P("group", "fsdp", None),
            P(("group", "fsdp"), None),
            P(("group", "fsdp"), None),
        ),
        out_specs=(
            P("fsdp", None),
            P("fsdp", None),
            P("group", "fsdp", None),
            P("group", "fsdp", None),
            P("group", "fsdp", None),
            P(("group", "fsdp"), None),
        ),
        check_vma=False,
    )
```

```python
import functools

import jax
import jax.numpy as jnp
from jax import lax
from jax.experimental import pallas as pl
from jax.experimental.pallas import tpu as pltpu
from jax.sharding import PartitionSpec as P

OUTER_RATE = 0.7
MOMENTUM = 0.9
INNER_RATE = 0.05
BETA_ONE = 0.9
BETA_TWO = 0.95
ADAM_EPS = 1e-08
DECAY = 0.1
ADAM_STEP = 100

TILE = 256
PIECES = 2
MESH = pl.DeviceIdType.MESH


def flip(index, slot):
    bit = 1
    while bit <= slot:
        if slot & bit:
            index = index + bit * (1 - 2 * lax.rem(lax.div(index, bit), 2))
        bit *= 2
    return index


def children(slot, n):
    top = slot & -slot if slot else n
    return [slot | 1 << at for at in reversed(range(n.bit_length() - 1)) if 1 << at < top]


def level_slots(level, n):
    return [slot for slot in range(n) if bin(slot).count("1") == level]


def exchange_kernel(
    n, scale,
    pg, anchor, moment, inputs, cot,
    grads_out, mean_out, input_grad_out,
    grads, input_grad,
    rows_in, cots, anchors, pg_core, pg_y, pg_pair, pg_own, anchor_own, moment_own, means,
    local_sem, out_sem,
    pg_send, pg_recv, x_send, x_recv, cot_send, cot_recv, tree_send, tree_recv,
    y_send, y_recv, core_send, core_recv, pass_send, pass_recv, mean_send, mean_recv,
):
    levels = n.bit_length() - 1
    tokens = inputs.shape[0]
    shard = anchor.shape[0]
    part = shard // 4
    me = lax.axis_index("fsdp")
    mine = lax.axis_index("group")
    y, core = lax.div(mine, 2), lax.rem(mine, 2)
    core_peer = 2 * y + 1 - core
    y_peer = 2 * (1 - y) + core
    piece_rows = part // PIECES

    def owner(slot):
        return flip(me, slot)

    def quarter(which):
        return pl.ds(pl.multiple_of(which * part, part), part)

    def piece_of(which, piece):
        return pl.ds(
            pl.multiple_of(which * part + piece * piece_rows, piece_rows), piece_rows
        )

    def local(src, dst, sem):
        return pltpu.make_async_copy(src, dst, local_sem.at[sem])

    def remote(src, dst, send, recv, fsdp, group):
        return pltpu.make_async_remote_copy(
            src_ref=src, dst_ref=dst, send_sem=send, recv_sem=recv,
            device_id={"group": group, "fsdp": fsdp}, device_id_type=MESH,
        )

    def shard_columns(index):
        return pl.ds(pl.multiple_of(index * shard, shard), shard)

    own_copies = [
        local(cot, cots.at[0], 0),
        local(pg.at[0, quarter(mine), :], pg_own.at[0], 1),
        local(pg.at[0, quarter(y_peer), :], pg_own.at[1], 2),
        local(anchor.at[quarter(mine), :], anchor_own, 3),
        local(moment.at[quarter(mine), :], moment_own, 4),
        local(inputs.at[:, shard_columns(me)], rows_in.at[0], 5),
    ]
    for copy in own_copies:
        copy.start()

    barrier = pltpu.get_barrier_semaphore()
    for step in range(1, n):
        pl.semaphore_signal(
            barrier, inc=1, device_id={"group": mine, "fsdp": owner(step)}, device_id_type=MESH
        )
    for peer in (core_peer, y_peer):
        pl.semaphore_signal(
            barrier, inc=1, device_id={"group": peer, "fsdp": me}, device_id_type=MESH
        )
    pl.semaphore_wait(barrier, n + 1)

    sent = []

    def send(copy):
        copy.start()
        sent.append(copy)

    def pg_core_copy(i, theirs):
        return remote(
            pg.at[0, quarter(theirs), :], pg_core.at[i], pg_send.at[i], pg_recv.at[i],
            me, core_peer,
        )

    core_of_y = 2 * (1 - y) + 1 - core
    pg_copies = [pg_core_copy(0, core_peer), pg_core_copy(1, core_of_y)]
    for i in (1, 0):
        send(pg_copies[i])

    def tree_copy(buffer, rows, slot, child, send_sem, recv_sem):
        return remote(
            buffer.at[slot, rows, :], buffer.at[child, rows, :],
            send_sem.at[child], recv_sem.at[child], flip(me, child - slot), mine,
        )

    def parent(slot):
        return slot & (slot - 1)

    def cot_copy(child):
        return tree_copy(cots, pl.ds(0, tokens), parent(child), child, cot_send, cot_recv)

    def anchor_copy(child, piece):
        return tree_copy(
            anchors, piece_of(mine, piece), parent(child), child,
            tree_send.at[piece], tree_recv.at[piece],
        )

    own_copies[0].wait()
    for child in children(0, n):
        send(cot_copy(child))

    def x_copy(slot):
        target = owner(slot)
        return remote(
            inputs.at[:, shard_columns(target)], rows_in.at[slot],
            x_send.at[slot], x_recv.at[slot], target, mine,
        )

    bulk = {
        0: [n // 2 + n // 4] + [slot for slot in level_slots(1, n)[::-1] if slot < n // 2],
    }
    bulk[1] = [slot for slot in range(n - 1, n // 2, -1) if slot not in bulk[0]]
    bulk[2] = [slot for slot in range(n - 1, 0, -1) if slot not in bulk[0] + bulk[1]]

    def send_bulk(turn):
        for slot in bulk[turn]:
            send(x_copy(slot))

    chunk = 32

    own_copies[2].wait()
    pg_copies[1].wait_recv()

    @pl.loop(0, part // chunk)
    def _(i):
        at = pl.ds(pl.multiple_of(i * chunk, chunk), chunk)
        pair = pg_own[1, at, :].astype(jnp.float32) + pg_core[1, at, :].astype(jnp.float32)
        pg_pair[at, :] = pair.astype(pg_pair.dtype)

    pg_y_copy = remote(pg_pair, pg_y, pg_send.at[2], pg_recv.at[2], me, y_peer)
    send(pg_y_copy)
    send_bulk(0)

    def cot_turn(level):
        for slot in level_slots(level, n):
            cot_copy(slot).wait_recv()
            for child in children(slot, n):
                send(cot_copy(child))

    def over(slot, piece, which, send_sem, recv_sem, peer):
        view = anchors.at[slot, piece_of(which, piece), :]
        return remote(view, view, send_sem.at[piece, slot], recv_sem.at[piece, slot], me, peer)

    def spread(slot, piece):
        send(over(slot, piece, mine, y_send, y_recv, y_peer))
        send(over(slot, piece, mine, core_send, core_recv, core_peer))

    def hand_on(level):
        for piece in range(PIECES):
            for slot in level_slots(level, n):
                over(slot, piece, mine, y_send, y_recv, y_peer).wait_recv()
                send(over(slot, piece, y_peer, pass_send, pass_recv, core_peer))

    def mean_copy(which, i, peer):
        view = means.at[quarter(which), :]
        return remote(view, view, mean_send.at[i], mean_recv.at[i], me, peer)

    out_copies = []

    def put_out(src, dst, at):
        copy = pltpu.make_async_copy(src, dst, out_sem.at[at])
        copy.start()
        out_copies.append(copy)

    def add_grads(slot):
        if slot == 0:
            own_copies[5].wait()
        else:
            x_copy(slot).wait_recv()

        @pl.loop(0, shard // TILE)
        def _(tile):
            at = pl.ds(pl.multiple_of(tile * TILE, TILE), TILE)
            term = lax.dot_general(
                rows_in[slot, :, at], cots[slot], (((0,), (0,)), ((), ())),
                preferred_element_type=jnp.float32,
            )
            if slot == 0:
                grads[at, :] = term
            else:
                grads[at, :] += term

    def put_input_grad(slot):
        for piece in range(PIECES):
            over(slot, piece, mine, core_send, core_recv, core_peer).wait_recv()
            over(slot, piece, y_peer, pass_send, pass_recv, core_peer).wait_recv()
        base = owner(slot) * shard

        @pl.loop(0, shard // TILE)
        def _(tile):
            at = pl.ds(pl.multiple_of(tile * TILE, TILE), TILE)
            term = lax.dot_general(
                cots[0], anchors[slot, at, :], (((1,), (1,)), ((), ())),
                preferred_element_type=jnp.float32,
            )
            columns = pl.ds(pl.multiple_of(base + tile * TILE, TILE), TILE)
            input_grad[:, columns] = (term * scale).astype(input_grad.dtype)

        put_out(
            input_grad.at[:, shard_columns(owner(slot))],
            input_grad_out.at[:, shard_columns(owner(slot))], slot,
        )

    for at in (1, 3, 4):
        own_copies[at].wait()
    pg_copies[0].wait_recv()
    pg_y_copy.wait_recv()

    @pl.loop(0, part // chunk)
    def _(i):
        at = pl.ds(pl.multiple_of(i * chunk, chunk), chunk)
        to = pl.ds(pl.multiple_of(mine * part + i * chunk, chunk), chunk)
        total = pg_own[0, at, :].astype(jnp.float32) + pg_core[0, at, :].astype(jnp.float32)
        mean = (total + pg_y[at, :].astype(jnp.float32)) / 4
        moved = MOMENTUM * moment_own[at, :] + mean
        updated = anchor_own[at, :].astype(jnp.float32) - OUTER_RATE * (mean + MOMENTUM * moved)
        anchors[0, to, :] = updated.astype(anchors.dtype)
        means[to, :] = mean.astype(means.dtype)

    for piece in range(PIECES):
        for child in children(0, n):
            send(anchor_copy(child, piece))
        spread(0, piece)
    send(mean_copy(mine, 0, core_peer))
    send(mean_copy(mine, 1, y_peer))
    cot_turn(1)

    late = bulk[0][::-1]
    for level in range(1, levels + 1):
        for piece in range(PIECES):
            for slot in level_slots(level, n):
                anchor_copy(slot, piece).wait_recv()
                for child in children(slot, n):
                    send(anchor_copy(child, piece))
                spread(slot, piece)
        if level < 3:
            send_bulk(level)
        if level < levels:
            cot_turn(level + 1)
        hand_on(level - 1)
        if level == 1:
            add_grads(0)
            mean_copy(mine, 1, y_peer).wait_recv()
            send(mean_copy(y_peer, 2, core_peer))
        if level >= 2:
            for slot in level_slots(level - 2, n):
                put_input_grad(slot)
        if level == 2:
            for slot in late[:-1]:
                add_grads(slot)
        if level == 3:
            add_grads(late[-1])

    mean_copy(mine, 0, core_peer).wait_recv()
    mean_copy(y_peer, 2, core_peer).wait_recv()
    put_out(means, mean_out, n)
    for slot in bulk[1]:
        add_grads(slot)
    for slot in level_slots(levels - 1, n):
        put_input_grad(slot)
    for slot in bulk[2][:0:-1]:
        add_grads(slot)
    hand_on(levels)
    add_grads(bulk[2][0])
    put_out(grads, grads_out, n + 1)
    put_input_grad(n - 1)
    for copy in sent:
        copy.wait_send()
    for copy in out_copies:
        copy.wait()


def exchange(n, scale, pg, anchor, moment, inputs, cot):
    tokens, width = inputs.shape
    shard, keys = anchor.shape
    part = shard // 4
    bf16, f32 = jnp.bfloat16, jnp.float32
    sem = pltpu.SemaphoreType.DMA
    return pl.pallas_call(
        functools.partial(exchange_kernel, n, scale),
        out_shape=(
            jax.ShapeDtypeStruct((shard, keys), f32),
            jax.ShapeDtypeStruct((shard, keys), bf16),
            jax.ShapeDtypeStruct((tokens, width), bf16),
        ),
        in_specs=[pl.BlockSpec(memory_space=pl.ANY)] * 5,
        out_specs=(pl.BlockSpec(memory_space=pl.ANY),) * 3,
        scratch_shapes=[
            pltpu.VMEM((shard, keys), f32),
            pltpu.VMEM((tokens, width), bf16),
            pltpu.VMEM((n, tokens, shard), bf16),
            pltpu.VMEM((n, tokens, keys), bf16),
            pltpu.VMEM((n, shard, keys), bf16),
            pltpu.VMEM((2, part, keys), bf16),
            pltpu.VMEM((part, keys), bf16),
            pltpu.VMEM((part, keys), bf16),
            pltpu.VMEM((2, part, keys), bf16),
            pltpu.VMEM((part, keys), bf16),
            pltpu.VMEM((part, keys), f32),
            pltpu.VMEM((shard, keys), bf16),
            sem((6,)), sem((n + 2,)),
            sem((3,)), sem((3,)),
            sem((n,)), sem((n,)),
            sem((n,)), sem((n,)),
            sem((PIECES, n)), sem((PIECES, n)),
            sem((PIECES, n)), sem((PIECES, n)),
            sem((PIECES, n)), sem((PIECES, n)),
            sem((PIECES, n)), sem((PIECES, n)),
            sem((3,)), sem((3,)),
        ],
        compiler_params=pltpu.CompilerParams(
            collective_id=0, has_side_effects=True, vmem_limit_bytes=51 * 2**20
        ),
        cost_estimate=pl.CostEstimate(
            flops=4 * tokens * width * keys,
            bytes_accessed=2 * (2 * tokens * width + 4 * shard * keys),
            transcendentals=0,
        ),
    )(pg, anchor, moment, inputs, cot)


def per_device(anchor, pseudo_grads, outer_moment, adam_first, adam_second, inputs, key_cotangent):
    scale = inputs.shape[1] ** (-0.5)
    raw, mean, input_grad = exchange(
        lax.axis_size("fsdp"), scale, pseudo_grads, anchor, outer_moment, inputs, key_cotangent
    )
    mean_delta = mean.astype(jnp.float32)
    grads = raw * scale
    new_moment = MOMENTUM * outer_moment + mean_delta
    new_anchor = (
        anchor.astype(jnp.float32) - OUTER_RATE * (mean_delta + MOMENTUM * new_moment)
    ).astype(jnp.bfloat16)
    correct_one = 1.0 - BETA_ONE**ADAM_STEP
    correct_two = 1.0 - BETA_TWO**ADAM_STEP
    first_moment = BETA_ONE * adam_first[0] + (1.0 - BETA_ONE) * grads
    second_moment = BETA_TWO * adam_second[0] + (1.0 - BETA_TWO) * grads * grads
    step_size = first_moment / correct_one / (jnp.sqrt(second_moment / correct_two) + ADAM_EPS)
    inner_weights = (
        new_anchor.astype(jnp.float32) * (1.0 - INNER_RATE * DECAY) - INNER_RATE * step_size
    ).astype(jnp.bfloat16)
    return (
        new_anchor,
        new_moment,
        inner_weights[None],
        first_moment[None],
        second_moment[None],
        input_grad,
    )


def solution(mesh):
    return jax.shard_map(
        per_device,
        mesh=mesh,
        in_specs=(
            P("fsdp", None),
            P("group", "fsdp", None),
            P("fsdp", None),
            P("group", "fsdp", None),
            P("group", "fsdp", None),
            P(("group", "fsdp"), None),
            P(("group", "fsdp"), None),
        ),
        out_specs=(
            P("fsdp", None),
            P("fsdp", None),
            P("group", "fsdp", None),
            P("group", "fsdp", None),
            P("group", "fsdp", None),
            P(("group", "fsdp"), None),
        ),
        check_vma=False,
    )
```

```python
import functools

import jax
import jax.numpy as jnp
from jax import lax
from jax.experimental import pallas as pl
from jax.experimental.pallas import tpu as pltpu
from jax.sharding import PartitionSpec as P

OUTER_RATE = 0.7
MOMENTUM = 0.9
INNER_RATE = 0.05
BETA_ONE = 0.9
BETA_TWO = 0.95
ADAM_EPS = 1e-08
DECAY = 0.1
ADAM_STEP = 100

TILE = 256
PIECES = 2
MESH = pl.DeviceIdType.MESH


def flip(index, slot):
    bit = 1
    while bit <= slot:
        if slot & bit:
            index = index + bit * (1 - 2 * lax.rem(lax.div(index, bit), 2))
        bit *= 2
    return index


def children(slot, n):
    top = slot & -slot if slot else n
    return [slot | 1 << at for at in reversed(range(n.bit_length() - 1)) if 1 << at < top]


def level_slots(level, n):
    return [slot for slot in range(n) if bin(slot).count("1") == level]


def exchange_kernel(
    n, scale,
    pg, anchor, moment, inputs, cot,
    grads_out, mean_out, input_grad_out,
    grads, input_grad,
    rows_in, cots, anchors, pg_core, pg_y, pg_pair, pg_own, anchor_own, moment_own, means,
    local_sem, out_sem,
    pg_send, pg_recv, x_send, x_recv, cot_send, cot_recv, tree_send, tree_recv,
    y_send, y_recv, core_send, core_recv, pass_send, pass_recv, mean_send, mean_recv,
):
    levels = n.bit_length() - 1
    tokens = inputs.shape[0]
    shard = anchor.shape[0]
    part = shard // 4
    me = lax.axis_index("fsdp")
    mine = lax.axis_index("group")
    y, core = lax.div(mine, 2), lax.rem(mine, 2)
    core_peer = 2 * y + 1 - core
    y_peer = 2 * (1 - y) + core
    piece_rows = part // PIECES

    def owner(slot):
        return flip(me, slot)

    def quarter(which):
        return pl.ds(pl.multiple_of(which * part, part), part)

    def piece_of(which, piece):
        return pl.ds(
            pl.multiple_of(which * part + piece * piece_rows, piece_rows), piece_rows
        )

    def local(src, dst, sem):
        return pltpu.make_async_copy(src, dst, local_sem.at[sem])

    def remote(src, dst, send, recv, fsdp, group):
        return pltpu.make_async_remote_copy(
            src_ref=src, dst_ref=dst, send_sem=send, recv_sem=recv,
            device_id={"group": group, "fsdp": fsdp}, device_id_type=MESH,
        )

    def shard_columns(index):
        return pl.ds(pl.multiple_of(index * shard, shard), shard)

    own_copies = [
        local(cot, cots.at[0], 0),
        local(pg.at[0, quarter(mine), :], pg_own.at[0], 1),
        local(pg.at[0, quarter(y_peer), :], pg_own.at[1], 2),
        local(anchor.at[quarter(mine), :], anchor_own, 3),
        local(moment.at[quarter(mine), :], moment_own, 4),
        local(inputs.at[:, shard_columns(me)], rows_in.at[0], 5),
    ]
    for copy in own_copies:
        copy.start()

    barrier = pltpu.get_barrier_semaphore()
    for step in range(1, n):
        pl.semaphore_signal(
            barrier, inc=1, device_id={"group": mine, "fsdp": owner(step)}, device_id_type=MESH
        )
    for peer in (core_peer, y_peer):
        pl.semaphore_signal(
            barrier, inc=1, device_id={"group": peer, "fsdp": me}, device_id_type=MESH
        )
    pl.semaphore_wait(barrier, n + 1)

    sent = []

    def send(copy):
        copy.start()
        sent.append(copy)

    def pg_core_copy(i, theirs):
        return remote(
            pg.at[0, quarter(theirs), :], pg_core.at[i], pg_send.at[i], pg_recv.at[i],
            me, core_peer,
        )

    core_of_y = 2 * (1 - y) + 1 - core
    pg_copies = [pg_core_copy(0, core_peer), pg_core_copy(1, core_of_y)]
    for i in (1, 0):
        send(pg_copies[i])

    def tree_copy(buffer, rows, slot, child, send_sem, recv_sem):
        return remote(
            buffer.at[slot, rows, :], buffer.at[child, rows, :],
            send_sem.at[child], recv_sem.at[child], flip(me, child - slot), mine,
        )

    def parent(slot):
        return slot & (slot - 1)

    def cot_copy(child):
        return tree_copy(cots, pl.ds(0, tokens), parent(child), child, cot_send, cot_recv)

    def anchor_copy(child, piece):
        return tree_copy(
            anchors, piece_of(mine, piece), parent(child), child,
            tree_send.at[piece], tree_recv.at[piece],
        )

    own_copies[0].wait()
    for child in children(0, n):
        send(cot_copy(child))

    def x_copy(slot):
        target = owner(slot)
        return remote(
            inputs.at[:, shard_columns(target)], rows_in.at[slot],
            x_send.at[slot], x_recv.at[slot], target, mine,
        )

    bulk = {
        0: [n // 2 + n // 4] + [slot for slot in level_slots(1, n)[::-1] if slot < n // 2],
    }
    bulk[1] = [slot for slot in range(n - 1, n // 2, -1) if slot not in bulk[0]]
    bulk[2] = [slot for slot in range(n - 1, 0, -1) if slot not in bulk[0] + bulk[1]]

    turns = (
        bulk[0][:1] + bulk[1][:1] + bulk[0][1:],
        bulk[1][1:] + bulk[2],
    )

    def send_bulk(turn):
        for slot in turns[turn]:
            send(x_copy(slot))

    chunk = 32

    own_copies[2].wait()
    pg_copies[1].wait_recv()

    @pl.loop(0, part // chunk)
    def _(i):
        at = pl.ds(pl.multiple_of(i * chunk, chunk), chunk)
        pair = pg_own[1, at, :].astype(jnp.float32) + pg_core[1, at, :].astype(jnp.float32)
        pg_pair[at, :] = pair.astype(pg_pair.dtype)

    pg_y_copy = remote(pg_pair, pg_y, pg_send.at[2], pg_recv.at[2], me, y_peer)
    send(pg_y_copy)
    send_bulk(0)

    def cot_turn(level):
        for slot in level_slots(level, n):
            cot_copy(slot).wait_recv()
            for child in children(slot, n):
                send(cot_copy(child))

    def over(slot, piece, which, send_sem, recv_sem, peer):
        view = anchors.at[slot, piece_of(which, piece), :]
        return remote(view, view, send_sem.at[piece, slot], recv_sem.at[piece, slot], me, peer)

    def spread(slot, piece):
        send(over(slot, piece, mine, y_send, y_recv, y_peer))
        send(over(slot, piece, mine, core_send, core_recv, core_peer))

    def hand_on(level):
        for piece in range(PIECES):
            for slot in level_slots(level, n):
                over(slot, piece, mine, y_send, y_recv, y_peer).wait_recv()
                send(over(slot, piece, y_peer, pass_send, pass_recv, core_peer))

    def mean_copy(which, i, peer):
        view = means.at[quarter(which), :]
        return remote(view, view, mean_send.at[i], mean_recv.at[i], me, peer)

    out_copies = []

    def put_out(src, dst, at):
        copy = pltpu.make_async_copy(src, dst, out_sem.at[at])
        copy.start()
        out_copies.append(copy)

    def add_grads(slot):
        if slot == 0:
            own_copies[5].wait()
        else:
            x_copy(slot).wait_recv()

        @pl.loop(0, shard // TILE)
        def _(tile):
            at = pl.ds(pl.multiple_of(tile * TILE, TILE), TILE)
            term = lax.dot_general(
                rows_in[slot, :, at], cots[slot], (((0,), (0,)), ((), ())),
                preferred_element_type=jnp.float32,
            )
            if slot == 0:
                grads[at, :] = term
            else:
                grads[at, :] += term

    def put_input_grad(slot):
        for piece in range(PIECES):
            over(slot, piece, mine, core_send, core_recv, core_peer).wait_recv()
            over(slot, piece, y_peer, pass_send, pass_recv, core_peer).wait_recv()
        base = owner(slot) * shard

        @pl.loop(0, shard // TILE)
        def _(tile):
            at = pl.ds(pl.multiple_of(tile * TILE, TILE), TILE)
            term = lax.dot_general(
                cots[0], anchors[slot, at, :], (((1,), (1,)), ((), ())),
                preferred_element_type=jnp.float32,
            )
            columns = pl.ds(pl.multiple_of(base + tile * TILE, TILE), TILE)
            input_grad[:, columns] = (term * scale).astype(input_grad.dtype)

        put_out(
            input_grad.at[:, shard_columns(owner(slot))],
            input_grad_out.at[:, shard_columns(owner(slot))], slot,
        )

    for at in (1, 3, 4):
        own_copies[at].wait()
    pg_copies[0].wait_recv()
    pg_y_copy.wait_recv()

    @pl.loop(0, part // chunk)
    def _(i):
        at = pl.ds(pl.multiple_of(i * chunk, chunk), chunk)
        to = pl.ds(pl.multiple_of(mine * part + i * chunk, chunk), chunk)
        total = pg_own[0, at, :].astype(jnp.float32) + pg_core[0, at, :].astype(jnp.float32)
        mean = (total + pg_y[at, :].astype(jnp.float32)) / 4
        moved = MOMENTUM * moment_own[at, :] + mean
        updated = anchor_own[at, :].astype(jnp.float32) - OUTER_RATE * (mean + MOMENTUM * moved)
        anchors[0, to, :] = updated.astype(anchors.dtype)
        means[to, :] = mean.astype(means.dtype)

    for piece in range(PIECES):
        for child in children(0, n):
            send(anchor_copy(child, piece))
        spread(0, piece)
    send(mean_copy(mine, 0, core_peer))
    send(mean_copy(mine, 1, y_peer))
    cot_turn(1)

    late = bulk[0][::-1]
    for level in range(1, levels + 1):
        for piece in range(PIECES):
            for slot in level_slots(level, n):
                anchor_copy(slot, piece).wait_recv()
                for child in children(slot, n):
                    send(anchor_copy(child, piece))
                spread(slot, piece)
        if level == 1:
            send_bulk(1)
        if level < levels:
            cot_turn(level + 1)
        hand_on(level - 1)
        if level == 1:
            add_grads(0)
            mean_copy(mine, 1, y_peer).wait_recv()
            send(mean_copy(y_peer, 2, core_peer))
        if level >= 2:
            for slot in level_slots(level - 2, n):
                put_input_grad(slot)
        if level == 2:
            for slot in late[:-1]:
                add_grads(slot)
        if level == 3:
            add_grads(late[-1])

    mean_copy(mine, 0, core_peer).wait_recv()
    mean_copy(y_peer, 2, core_peer).wait_recv()
    put_out(means, mean_out, n)
    for slot in bulk[1]:
        add_grads(slot)
    for slot in level_slots(levels - 1, n):
        put_input_grad(slot)
    for slot in bulk[2][:0:-1]:
        add_grads(slot)
    hand_on(levels)
    add_grads(bulk[2][0])
    put_out(grads, grads_out, n + 1)
    put_input_grad(n - 1)
    for copy in sent:
        copy.wait_send()
    for copy in out_copies:
        copy.wait()


def exchange(n, scale, pg, anchor, moment, inputs, cot):
    tokens, width = inputs.shape
    shard, keys = anchor.shape
    part = shard // 4
    bf16, f32 = jnp.bfloat16, jnp.float32
    sem = pltpu.SemaphoreType.DMA
    return pl.pallas_call(
        functools.partial(exchange_kernel, n, scale),
        out_shape=(
            jax.ShapeDtypeStruct((shard, keys), f32),
            jax.ShapeDtypeStruct((shard, keys), bf16),
            jax.ShapeDtypeStruct((tokens, width), bf16),
        ),
        in_specs=[pl.BlockSpec(memory_space=pl.ANY)] * 5,
        out_specs=(pl.BlockSpec(memory_space=pl.ANY),) * 3,
        scratch_shapes=[
            pltpu.VMEM((shard, keys), f32),
            pltpu.VMEM((tokens, width), bf16),
            pltpu.VMEM((n, tokens, shard), bf16),
            pltpu.VMEM((n, tokens, keys), bf16),
            pltpu.VMEM((n, shard, keys), bf16),
            pltpu.VMEM((2, part, keys), bf16),
            pltpu.VMEM((part, keys), bf16),
            pltpu.VMEM((part, keys), bf16),
            pltpu.VMEM((2, part, keys), bf16),
            pltpu.VMEM((part, keys), bf16),
            pltpu.VMEM((part, keys), f32),
            pltpu.VMEM((shard, keys), bf16),
            sem((6,)), sem((n + 2,)),
            sem((3,)), sem((3,)),
            sem((n,)), sem((n,)),
            sem((n,)), sem((n,)),
            sem((PIECES, n)), sem((PIECES, n)),
            sem((PIECES, n)), sem((PIECES, n)),
            sem((PIECES, n)), sem((PIECES, n)),
            sem((PIECES, n)), sem((PIECES, n)),
            sem((3,)), sem((3,)),
        ],
        compiler_params=pltpu.CompilerParams(
            collective_id=0, has_side_effects=True, vmem_limit_bytes=51 * 2**20
        ),
        cost_estimate=pl.CostEstimate(
            flops=4 * tokens * width * keys,
            bytes_accessed=2 * (2 * tokens * width + 4 * shard * keys),
            transcendentals=0,
        ),
    )(pg, anchor, moment, inputs, cot)


def per_device(anchor, pseudo_grads, outer_moment, adam_first, adam_second, inputs, key_cotangent):
    scale = inputs.shape[1] ** (-0.5)
    raw, mean, input_grad = exchange(
        lax.axis_size("fsdp"), scale, pseudo_grads, anchor, outer_moment, inputs, key_cotangent
    )
    mean_delta = mean.astype(jnp.float32)
    grads = raw * scale
    new_moment = MOMENTUM * outer_moment + mean_delta
    new_anchor = (
        anchor.astype(jnp.float32) - OUTER_RATE * (mean_delta + MOMENTUM * new_moment)
    ).astype(jnp.bfloat16)
    correct_one = 1.0 - BETA_ONE**ADAM_STEP
    correct_two = 1.0 - BETA_TWO**ADAM_STEP
    first_moment = BETA_ONE * adam_first[0] + (1.0 - BETA_ONE) * grads
    second_moment = BETA_TWO * adam_second[0] + (1.0 - BETA_TWO) * grads * grads
    step_size = first_moment / correct_one / (jnp.sqrt(second_moment / correct_two) + ADAM_EPS)
    inner_weights = (
        new_anchor.astype(jnp.float32) * (1.0 - INNER_RATE * DECAY) - INNER_RATE * step_size
    ).astype(jnp.bfloat16)
    return (
        new_anchor,
        new_moment,
        inner_weights[None],
        first_moment[None],
        second_moment[None],
        input_grad,
    )


def solution(mesh):
    return jax.shard_map(
        per_device,
        mesh=mesh,
        in_specs=(
            P("fsdp", None),
            P("group", "fsdp", None),
            P("fsdp", None),
            P("group", "fsdp", None),
            P("group", "fsdp", None),
            P(("group", "fsdp"), None),
            P(("group", "fsdp"), None),
        ),
        out_specs=(
            P("fsdp", None),
            P("fsdp", None),
            P("group", "fsdp", None),
            P("group", "fsdp", None),
            P("group", "fsdp", None),
            P(("group", "fsdp"), None),
        ),
        check_vma=False,
    )
```
